32 devices in a mesh: slab: 4 (over y, x), brick: 8 (over z, core).
Axes of the slice: x: 2, y: 2, z: 4, core: 2. Of those that a mesh axis runs over, the one named last changes fastest.
Arguments:
- positions: float32 [3, 4096], P(None, ('slab', 'brick')), may hold values from -0.45 to 15.85, as said below
- species: int32 [4096], P(('slab', 'brick')), may hold values from 0 to 88
- neighbour_slot: int32 [4096, 32], P(('slab', 'brick')), may hold values from 0 to 415, as said below
- neighbour_count: int32 [4096], P(('slab', 'brick')), may hold values from 22 to 32
- face_rows: int32 [32, 4, 64], P(('slab', 'brick')), may hold values from 0 to 127, as said below
- edge_rows: int32 [32, 4, 8], P(('slab', 'brick')), may hold values from 0 to 127, as said below
- embedding: bfloat16 [89, 128], replicated, may hold values from -6 to 6
- radial_first: bfloat16 [2, 8, 64], replicated, may hold values from -24 to 24
- radial_hidden: bfloat16 [2, 2, 64, 64], replicated, may hold values from -0.75 to 0.75
- radial_last_one: bfloat16 [64, 384], replicated, may hold values from -0.75 to 0.75
- radial_last_two: bfloat16 [64, 896], replicated, may hold values from -0.75 to 0.75
- product_weight: bfloat16 [2, 89, 1024], replicated, may hold values from -4 to 4
- mix_weight: bfloat16 [2, 128, 128], replicated, may hold values from -0.5 to 0.5
- skip_weight: bfloat16 [2, 128, 128], replicated, may hold values from -0.5 to 0.5
- equi_weight: bfloat16 [89, 512], replicated, may hold values from -4 to 4
- equi_mix: bfloat16 [2, 128, 128], replicated, may hold values from -0.5 to 0.5
- atom_reference: float32 [89], replicated, may hold values from -6 to 6
- readout_weight: bfloat16 [128], replicated, may hold values from -0.5 to 0.5
- head_weight: bfloat16 [128, 16], replicated, may hold values from -0.5 to 0.5
- final_weight: bfloat16 [16], replicated, may hold values from -1.5 to 1.5
Outputs:
- atom_energy: float32 [4096], P(('slab', 'brick'))
- forces: float32 [3, 4096], P(None, ('slab', 'brick'))
The draws below stay inside these ranges and needn't reach their ends.
Inputs may be any that keep to these rules, and one draw needn't show every extreme that they name: `positions`: atoms sit on a lattice of spacing 2.2 with 4 x 8 x 4 sites a device, each within 0.45 of its site in every component; the cell is periodic along x and z and walled along y. `neighbour_slot`: live slots come first; slots past an atom's count also name atoms within the cutoff of 6. `face_rows`: rows of one device, distinct within each list. `edge_rows`: rows of one device, distinct within each list.
All inputs are finite; a program needn't handle non-finite values.
Results may differ from the reference program's by a relative error of at most 0.019.
Values may be sent and summed in bfloat16 or wider, within the bound.
A program may use at most 128 MiB of HBM per device.

```python
import math
import jax
import jax.numpy as jnp
import numpy as np
from jax import lax

C = 128
RAD = 64
BESSEL = 8
HEAD = 16
SPECIES = 89
NBR = 32
LXZ = 4
LY = 8
A_DEV = 128
GF = 64
GE = 8
BRICKS = 32
ATOMS = 4096
N_SLAB = 4
N_BRICK = 8


SPACING = 2.2


LATTICE_STEPS = tuple([(step_x, step_y, step_z) for step_x in (-1, 0, 1) for step_y in (-1, 0, 1) for step_z in (-1, 0, 1) if (step_x, step_y, step_z) != (0, 0, 0)] + [(2, 0, 0), (-2, 0, 0), (0, 2, 0), (0, -2, 0), (0, 0, 2), (0, 0, -2)])


def site_number(coord_x, coord_y, coord_z):
    return (coord_x * LY + coord_y) * LXZ + coord_z


def lattice_order(key):
    keys = jax.random.split(jax.random.fold_in(key, 17), BRICKS)
    placed = jax.vmap(lambda single: jax.random.permutation(single, A_DEV))(keys).astype(jnp.int32)
    sites_of = jnp.argsort(placed, axis=1, stable=True).astype(jnp.int32)
    return (placed, sites_of)


def site_coords(sites):
    return (sites // (LY * LXZ), sites // LXZ % LY, sites % LXZ)


def neighbour_plan(key):
    placed, sites_of = lattice_order(key)
    sites = jnp.arange(A_DEV, dtype=jnp.int32)
    coord_x, coord_y, coord_z = site_coords(sites)
    steps = jnp.array(LATTICE_STEPS, dtype=jnp.int32)
    target_x = coord_x[:, None] + steps[None, :, 0]
    raw_y = coord_y[:, None] + steps[None, :, 1]
    target_z = coord_z[:, None] + steps[None, :, 2]
    inside = (raw_y >= 0) & (raw_y < LY)
    target_y = jnp.where(inside, raw_y, coord_y[:, None] - steps[None, :, 1])
    brick_step = (target_x >= LXZ).astype(jnp.int32) - (target_x < 0).astype(jnp.int32)
    slab_step = (target_z >= LXZ).astype(jnp.int32) - (target_z < 0).astype(jnp.int32)
    local_x = target_x - brick_step * LXZ
    local_z = target_z - slab_step * LXZ
    face_plus_x = (local_x * LY + target_y) * LXZ + local_z
    face_minus_x = ((local_x - (LXZ - 2)) * LY + target_y) * LXZ + local_z
    face_plus_z = (local_z * LXZ + local_x) * LY + target_y
    face_minus_z = ((local_z - (LXZ - 2)) * LXZ + local_x) * LY + target_y
    face_slot = jnp.where(brick_step == 1, A_DEV + face_plus_x, jnp.where(brick_step == -1, A_DEV + GF + face_minus_x, jnp.where(slab_step == 1, A_DEV + 2 * GF + face_plus_z, A_DEV + 3 * GF + face_minus_z)))
    corner = jnp.where(slab_step == 1, jnp.where(brick_step == 1, 0, 1), jnp.where(brick_step == 1, 2, 3))
    corner_slot = A_DEV + 4 * GF + corner * GE + target_y
    own_site = site_number(local_x, target_y, local_z)
    own_slot = placed[:, own_site]
    is_own = (brick_step == 0) & (slab_step == 0)
    is_corner = (brick_step != 0) & (slab_step != 0)
    by_site = jnp.where(is_own[None], own_slot, jnp.where(is_corner, corner_slot, face_slot)[None])
    scores = jax.random.randint(jax.random.fold_in(key, 23), (BRICKS, A_DEV, NBR), 0, 1 << 20, dtype=jnp.int32)
    ranking = jnp.where(inside[None], 0, 1 << 26) + scores * NBR + jnp.arange(NBR, dtype=jnp.int32)
    ordering = jnp.argsort(ranking, axis=2, stable=True)
    by_site = jnp.take_along_axis(by_site, ordering, axis=2)
    counted = jnp.sum(inside.astype(jnp.int32), axis=1)
    slots_rows = jnp.take_along_axis(by_site, sites_of[:, :, None], axis=1)
    count_rows = counted[sites_of]
    return (slots_rows.astype(jnp.int32), count_rows.astype(jnp.int32))


def draw_neighbour_slot(key, part):
    return neighbour_plan(key)[0].reshape(ATOMS, NBR)


def draw_neighbour_count(key, part):
    return neighbour_plan(key)[1].reshape(ATOMS)


def draw_face_rows(key, part):
    placed = lattice_order(key)[0]
    listing = jnp.arange(GF, dtype=jnp.int32)
    layer_a = listing // (LY * LXZ)
    middle_y = listing // LXZ % LY
    lowest_z = listing % LXZ
    layer_b = listing // (LXZ * LY)
    middle_x = listing // LY % LXZ
    lowest_y = listing % LY
    tables = [site_number(layer_a, middle_y, lowest_z), site_number(LXZ - 2 + layer_a, middle_y, lowest_z), site_number(middle_x, lowest_y, layer_b), site_number(middle_x, lowest_y, LXZ - 2 + layer_b)]
    return jnp.stack([placed[:, table] for table in tables], axis=1).astype(jnp.int32)


def draw_edge_rows(key, part):
    placed = lattice_order(key)[0]
    along_y = jnp.arange(GE, dtype=jnp.int32)
    tables = []
    for slab_step, brick_step in ((1, 1), (1, -1), (-1, 1), (-1, -1)):
        corner_x = 0 if brick_step == 1 else LXZ - 1
        corner_z = 0 if slab_step == 1 else LXZ - 1
        tables.append(placed[:, site_number(corner_x, along_y, corner_z)])
    return jnp.stack(tables, axis=1).astype(jnp.int32)


def draw_positions(key, part):
    sites_of = lattice_order(key)[1]
    coord_x, coord_y, coord_z = site_coords(sites_of)
    lattice = jnp.stack([coord_x, coord_y, coord_z], axis=1).astype(jnp.float32) * SPACING
    noise_key = jax.random.fold_in(key, 29)
    jitter = 0.15 * jax.random.truncated_normal(noise_key, -3.0, 3.0, lattice.shape, jnp.float32)
    return (lattice + jitter).transpose(1, 0, 2).reshape(3, ATOMS)


def place_ends(values, own_key, low, high):
    spot = [jax.random.randint(jax.random.fold_in(own_key, axis), (), 0, length) for axis, length in enumerate(values.shape)]
    longest = values.shape.index(max(values.shape))
    beside = spot[:longest] + [(spot[longest] + 1) % values.shape[longest]] + spot[longest + 1:]
    return values.at[tuple(spot)].set(low).at[tuple(beside)].set(high)


def cumulative_ranks(count, slope):
    loads = [(1 << 20) // math.isqrt(rank ** slope) + 1 for rank in range(1, count + 1)]
    scale = 1 + sum(loads) // (1 << 30)
    return np.cumsum(np.array([max(1, weight // scale) for weight in loads]))


def skewed_ids(rng, shape, number_of, slope):
    table = cumulative_ranks(number_of, slope)
    ticket = jax.random.randint(jax.random.fold_in(rng, 1), shape, 0, int(table[number_of - 1]))
    grade = jnp.searchsorted(jnp.asarray(table, jnp.int32), ticket, side="right")
    return jax.random.permutation(jax.random.fold_in(rng, 2), number_of)[grade].astype(jnp.int32)


def gaussian(key, dims, width, most, held_as=jnp.bfloat16):
    drawn = width * jax.random.normal(key, dims, jnp.float32)
    return jnp.clip(drawn, min=-most, max=most).astype(held_as)


def setup_inputs(seed: int = 0) -> dict:
    seeds = jax.random.split(jax.random.key(seed), 21)
    positions = draw_positions(jax.random.fold_in(seeds[20], 71), 0)
    species = place_ends(skewed_ids(seeds[1], (ATOMS,), SPECIES, 2), jax.random.fold_in(seeds[1], 3), 0, SPECIES - 1).astype(jnp.int32)
    neighbour_slot = draw_neighbour_slot(jax.random.fold_in(seeds[20], 71), 0)
    neighbour_count = draw_neighbour_count(jax.random.fold_in(seeds[20], 71), 0)
    face_rows = draw_face_rows(jax.random.fold_in(seeds[20], 71), 0)
    edge_rows = draw_edge_rows(jax.random.fold_in(seeds[20], 71), 0)
    embedding = gaussian(seeds[6], (SPECIES, C), 1.0, 6.0)
    radial_first = gaussian(seeds[7], (2, BESSEL, RAD), 4.0, 24.0)
    radial_hidden = gaussian(seeds[8], (2, 2, RAD, RAD), RAD ** -0.5, 0.75)
    radial_last_one = gaussian(seeds[9], (RAD, 3 * C), RAD ** -0.5, 0.75)
    radial_last_two = gaussian(seeds[10], (RAD, 7 * C), RAD ** -0.5, 0.75)
    product_weight = gaussian(seeds[11], (2, SPECIES, 8 * C), 2 ** -0.5, 4.0)
    mix_weight = gaussian(seeds[12], (2, C, C), C ** -0.5, 0.5)
    skip_weight = gaussian(seeds[13], (2, C, C), C ** -0.5, 0.5)
    equi_weight = gaussian(seeds[14], (SPECIES, 4 * C), 2 ** -0.5, 4.0)
    equi_mix = gaussian(seeds[15], (2, C, C), C ** -0.5, 0.5)
    atom_reference = gaussian(seeds[16], (SPECIES,), 1.0, 6.0, jnp.float32)
    readout_weight = gaussian(seeds[17], (C,), C ** -0.5, 0.5)
    head_weight = gaussian(seeds[18], (C, HEAD), C ** -0.5, 0.5)
    final_weight = gaussian(seeds[19], (HEAD,), HEAD ** -0.5, 1.5)
    return {"positions": positions, "species": species, "neighbour_slot": neighbour_slot, "neighbour_count": neighbour_count, "face_rows": face_rows, "edge_rows": edge_rows, "embedding": embedding, "radial_first": radial_first, "radial_hidden": radial_hidden, "radial_last_one": radial_last_one, "radial_last_two": radial_last_two, "product_weight": product_weight, "mix_weight": mix_weight, "skip_weight": skip_weight, "equi_weight": equi_weight, "equi_mix": equi_mix, "atom_reference": atom_reference, "readout_weight": readout_weight, "head_weight": head_weight, "final_weight": final_weight}


SPACING = 2.2
CUTOFF = 6.0
DIRECTIONS = ((0, 1), (0, -1), (1, 0), (-1, 0), (1, 1), (1, -1), (-1, 1), (-1, -1))
LEADING = (((0,), (0,)), ((), ()))

def harmonics(heading):
    along_x, along_y, along_z = (heading[0], heading[1], heading[2])
    root_three = math.sqrt(3.0)
    root_five = math.sqrt(5.0)
    root_fifteen = math.sqrt(15.0)
    return jnp.stack([jnp.ones_like(along_x), root_three * along_x, root_three * along_y, root_three * along_z, root_fifteen * along_x * along_y, root_fifteen * along_y * along_z, 0.5 * root_five * (3.0 * along_z * along_z - 1.0), root_fifteen * along_x * along_z, 0.5 * root_fifteen * (along_x * along_x - along_y * along_y)])

def block_layer(own_pos, slots, counts, onehot, own_feat, ext_pos, ext_feat, weights, extra):
    radial_first, radial_hidden, radial_last, product_weight, mix_weight, skip_weight = weights
    atoms_here, slot_count = slots.shape
    channels = skip_weight.shape[1]
    nearby = jnp.take(ext_pos, slots, axis=1)
    relative = nearby - own_pos[:, :, None]
    distance = jnp.sqrt(lax.optimization_barrier(jnp.sum(relative * relative, axis=0)))
    heading = relative / distance[None]
    scaled = distance / CUTOFF
    fifth_power = scaled ** 5
    envelope = 1.0 - 21.0 * fifth_power + 35.0 * fifth_power * scaled - 15.0 * fifth_power * scaled * scaled
    flat_dist = distance.reshape(1, -1)
    flat_env = envelope.reshape(1, -1)
    orders = jnp.arange(1, radial_first.shape[0] + 1).astype(jnp.float32)[:, None] * (math.pi / CUTOFF)
    bessel_basis = (math.sqrt(2.0 / CUTOFF) * jnp.sin(flat_dist * orders) / flat_dist * flat_env).astype(jnp.bfloat16)
    hidden_one = jax.nn.silu(lax.dot_general(radial_first, bessel_basis, LEADING, preferred_element_type=jnp.float32)).astype(jnp.bfloat16)
    hidden_two = jax.nn.silu(lax.dot_general(radial_hidden[0], hidden_one, LEADING, preferred_element_type=jnp.float32)).astype(jnp.bfloat16)
    hidden_three = jax.nn.silu(lax.dot_general(radial_hidden[1], hidden_two, LEADING, preferred_element_type=jnp.float32)).astype(jnp.bfloat16)
    radial = lax.dot_general(hidden_three, radial_last, LEADING, preferred_element_type=jnp.float32).astype(jnp.bfloat16)
    path_count = radial_last.shape[1] // channels
    radial = radial.reshape(atoms_here, slot_count, path_count, channels)

    def path(index):
        return radial[:, :, index, :].astype(jnp.float32)
    slot_live = (jnp.arange(slot_count)[None, :] < counts[:, None]).astype(jnp.float32) / math.sqrt(slot_count)
    angular = harmonics(heading) * slot_live[None]
    spread = jnp.moveaxis(angular, 0, 2)[:, :, :, None]
    plain_weight = angular[0][:, :, None]
    gathered = jnp.take(ext_feat, slots, axis=0)
    if extra is not None:
        moments = []
        for degree in range(3):
            weighted = path(degree) * gathered
            first_row = degree * degree
            last_row = (degree + 1) * (degree + 1)
            moments.append(lax.optimization_barrier(jnp.sum(spread[:, :, first_row:last_row] * weighted[:, :, None, :], axis=1)))
        scalar = moments[0][:, 0, :]
        vector = moments[1]
        tensor = moments[2]
    else:
        parts = gathered.reshape(atoms_here, slot_count, 9, channels)
        plain = parts[:, :, 0, :]
        first_part = parts[:, :, 1:4, :]
        second_part = parts[:, :, 4:9, :]
        dot_one = lax.optimization_barrier(jnp.sum(spread[:, :, 1:4] * first_part, axis=2))
        dot_two = lax.optimization_barrier(jnp.sum(spread[:, :, 4:9] * second_part, axis=2))
        scalar = lax.optimization_barrier(jnp.sum(plain_weight * path(0) * plain + path(1) * dot_one + path(2) * dot_two, axis=1))
        vector = lax.optimization_barrier(jnp.sum(spread[:, :, 1:4] * (path(3) * plain)[:, :, None, :] + plain_weight[:, :, :, None] * path(4)[:, :, None, :] * first_part, axis=1))
        tensor = lax.optimization_barrier(jnp.sum(spread[:, :, 4:9] * (path(5) * plain)[:, :, None, :] + plain_weight[:, :, :, None] * path(6)[:, :, None, :] * second_part, axis=1))
    norm_one = lax.optimization_barrier(jnp.sum(vector * vector, axis=1))
    norm_two = lax.optimization_barrier(jnp.sum(tensor * tensor, axis=1))
    along_x, along_y, along_z = (vector[:, 0], vector[:, 1], vector[:, 2])
    root_third = 1.0 / math.sqrt(3.0)
    diagonal_x = tensor[:, 4] - root_third * tensor[:, 2]
    diagonal_y = -tensor[:, 4] - root_third * tensor[:, 2]
    diagonal_z = 2.0 * root_third * tensor[:, 2]
    coupled = 3.0 / math.sqrt(15.0) * (diagonal_x * along_x * along_x + diagonal_y * along_y * along_y + diagonal_z * along_z * along_z + 2.0 * (tensor[:, 0] * along_x * along_y + tensor[:, 1] * along_y * along_z + tensor[:, 3] * along_x * along_z))
    invariants = [scalar, scalar * scalar, norm_one, norm_two, scalar * scalar * scalar, scalar * norm_one, scalar * norm_two, coupled]
    select = jnp.dot(onehot, product_weight, preferred_element_type=jnp.float32)
    mixed = invariants[0] * select[:, :channels]
    for which_term in range(1, 8):
        mixed = mixed + invariants[which_term] * select[:, which_term * channels:(which_term + 1) * channels]
    mixed = mixed.astype(jnp.bfloat16)
    scalar_out = jnp.dot(mixed, mix_weight, preferred_element_type=jnp.float32) + jnp.dot(own_feat.astype(jnp.bfloat16), skip_weight, preferred_element_type=jnp.float32)
    if extra is None:
        return scalar_out
    equi_weight, equi_mix = extra
    gates = jnp.dot(onehot, equi_weight, preferred_element_type=jnp.float32)
    vec_gate = gates[:, None, :channels] + gates[:, None, channels:2 * channels] * scalar[:, None, :]
    ten_gate = gates[:, None, 2 * channels:3 * channels] + gates[:, None, 3 * channels:] * scalar[:, None, :]
    vec_in = (vector * vec_gate).astype(jnp.bfloat16)
    ten_in = (tensor * ten_gate).astype(jnp.bfloat16)
    vec_out = jnp.dot(vec_in.reshape(-1, channels), equi_mix[0], preferred_element_type=jnp.float32)
    ten_out = jnp.dot(ten_in.reshape(-1, channels), equi_mix[1], preferred_element_type=jnp.float32)
    whole = jnp.concatenate([scalar_out[:, None, :], vec_out.reshape(atoms_here, 3, channels), ten_out.reshape(atoms_here, 5, channels)], axis=1)
    return whole.reshape(atoms_here, 9 * channels)

def interact(own_pos, slots, counts, onehot, own_feat, ext_pos, ext_feat, weights, extra):
    atoms_here = own_pos.shape[1]
    block_rows = 32 if atoms_here % 32 == 0 else atoms_here

    def one_block(number):
        first_atom = number * block_rows

        def cut_rows(array, axis_dim):
            return lax.dynamic_slice_in_dim(array, first_atom, block_rows, axis_dim)
        return block_layer(cut_rows(own_pos, 1), cut_rows(slots, 0), cut_rows(counts, 0), cut_rows(onehot, 0), cut_rows(own_feat, 0), ext_pos, ext_feat, weights, extra)
    outputs = lax.map(jax.checkpoint(one_block), jnp.arange(atoms_here // block_rows, dtype=jnp.int32))
    return outputs.reshape(atoms_here, -1)

def energies(feat_one, feat_two, onehot, atom_reference, readout_weight, head_weight, final_weight):
    first_term = jnp.dot(feat_one.astype(jnp.bfloat16), readout_weight, preferred_element_type=jnp.float32)
    readout = jax.nn.silu(jnp.dot(feat_two.astype(jnp.bfloat16), head_weight, preferred_element_type=jnp.float32))
    second_term = lax.optimization_barrier(jnp.sum(readout * final_weight.astype(jnp.float32), axis=1))
    base_term = jnp.dot(onehot.astype(jnp.float32), atom_reference, precision=lax.Precision.HIGHEST)
    return base_term + first_term + second_term

def layer_params(layer_index, radial_first, radial_hidden, radial_last, product_weight, mix_weight, skip_weight):
    return (radial_first[layer_index], radial_hidden[layer_index], radial_last, product_weight[layer_index], mix_weight[layer_index], skip_weight[layer_index])

def ghost_rows(values, face_table, edge_table):
    pieces = []
    for direction in range(8):
        slab_step, brick_step = DIRECTIONS[direction]
        source = jnp.roll(values, (-slab_step, -brick_step), (0, 1))
        table = face_table[:, :, direction] if direction < 4 else edge_table[:, :, direction - 4]
        rows_now = jnp.roll(table, (-slab_step, -brick_step), (0, 1))
        pieces.append(jax.vmap(jax.vmap(lambda source_block, chosen: jnp.take(source_block, chosen, axis=0)))(source, rows_now))
    return pieces

def reference(positions, species, neighbour_slot, neighbour_count, face_rows, edge_rows, embedding, radial_first, radial_hidden, radial_last_one, radial_last_two, product_weight, mix_weight, skip_weight, equi_weight, equi_mix, atom_reference, readout_weight, head_weight, final_weight):
    devices_all = N_SLAB * N_BRICK
    channels = embedding.shape[1]
    face_table = face_rows.reshape(N_SLAB, N_BRICK, 4, GF)
    edge_table = edge_rows.reshape(N_SLAB, N_BRICK, 4, GE)
    slots_all = neighbour_slot.reshape(devices_all, A_DEV, NBR)
    counts_all = neighbour_count.reshape(devices_all, A_DEV)
    kinds = jnp.arange(SPECIES, dtype=jnp.int32)
    onehot = (species.reshape(devices_all, A_DEV)[:, :, None] == kinds).astype(jnp.bfloat16)
    start_feat = jnp.dot(onehot, embedding, preferred_element_type=jnp.float32)
    weights_one = layer_params(0, radial_first, radial_hidden, radial_last_one, product_weight, mix_weight, skip_weight)
    weights_two = layer_params(1, radial_first, radial_hidden, radial_last_two, product_weight, mix_weight, skip_weight)
    extra_one = (equi_weight, equi_mix)
    brick_span = LXZ * SPACING

    def extend_feat(features):
        grid = features.reshape(N_SLAB, N_BRICK, A_DEV, features.shape[-1])
        pieces = ghost_rows(grid, face_table, edge_table)
        return jnp.concatenate([grid] + pieces, axis=2).reshape(devices_all, -1, features.shape[-1])

    def extend_pos(own_all):
        grid = own_all.reshape(N_SLAB, N_BRICK, 3, A_DEV).transpose(0, 1, 3, 2)
        pieces = ghost_rows(grid, face_table, edge_table)
        shifted = []
        for direction in range(8):
            slab_step, brick_step = DIRECTIONS[direction]
            offset_vec = jnp.array([brick_step * brick_span, 0.0, slab_step * brick_span], jnp.float32)
            shifted.append(pieces[direction] + offset_vec)
        whole = jnp.concatenate([grid] + shifted, axis=2)
        return whole.transpose(0, 1, 3, 2).reshape(devices_all, 3, -1)

    def total_energy(flat_pos):
        own_all = flat_pos.reshape(3, devices_all, A_DEV).transpose(1, 0, 2)
        ext_pos = extend_pos(own_all)
        ext_start = extend_feat(start_feat)

        def first_device(bundle):
            return interact(bundle[0], bundle[1], bundle[2], bundle[3], bundle[4], bundle[5], bundle[6], weights_one, extra_one)
        feat_one = lax.map(first_device, (own_all, slots_all, counts_all, onehot, start_feat, ext_pos, ext_start))
        feat_round = lax.optimization_barrier(feat_one.astype(jnp.bfloat16)).astype(jnp.float32)
        ext_one = extend_feat(feat_round)

        def second_device(bundle):
            own_scalar = bundle[4][:, :channels]
            feat_two = interact(bundle[0], bundle[1], bundle[2], bundle[3], own_scalar, bundle[5], bundle[6], weights_two, None)
            return energies(own_scalar, feat_two, bundle[3], atom_reference, readout_weight, head_weight, final_weight)
        per_atom = lax.map(second_device, (own_all, slots_all, counts_all, onehot, feat_round, ext_pos, ext_one))
        per_atom = per_atom.reshape(-1)
        return (jnp.sum(per_atom), per_atom)
    total, back_fn, atom_energy = jax.vjp(total_energy, positions, has_aux=True)
    gradient = back_fn(jnp.ones_like(total))[0]
    return (atom_energy, -gradient)
```

```python
import functools
import math

import jax
import jax.numpy as jnp
from jax import lax
from jax.experimental import pallas as pl
from jax.experimental.pallas import tpu as pltpu
from jax.sharding import PartitionSpec as P

LXZ = 4
SPACING = 2.2
CUTOFF = 6.0
DIRECTIONS = ((0, 1), (0, -1), (1, 0), (-1, 0), (1, 1), (1, -1), (-1, 1), (-1, -1))
MESH = pl.DeviceIdType.MESH
F32 = jnp.float32
BF16 = jnp.bfloat16
GROUP = 4
EDGE = 16
CHUNK = 16
NN = (((1,), (0,)), ((), ()))
NT = (((1,), (1,)), ((), ()))
TN = (((0,), (0,)), ((), ()))


def mm(a, b, dims=NN):
    return lax.dot_general(a, b, dims, preferred_element_type=F32)


@jax.custom_vjp
def mapped(x, weight):
    return mm(x, weight)


def mapped_fwd(x, weight):
    return mm(x, weight), weight


def mapped_bwd(weight, ct):
    return mm(ct.astype(BF16), weight, NT).astype(BF16), jnp.zeros_like(weight)


mapped.defvjp(mapped_fwd, mapped_bwd)


def geometry(rx, ry, rz, orders):
    dist = jnp.sqrt(rx * rx + ry * ry + rz * rz)
    inv = 1.0 / dist
    ux, uy, uz = rx * inv, ry * inv, rz * inv
    x = dist * (1.0 / CUTOFF)
    x2 = x * x
    x5 = x2 * x2 * x
    env = 1.0 - 21.0 * x5 + 35.0 * x5 * x - 15.0 * x5 * x2
    basis = jnp.sin(dist * orders) * (math.sqrt(2.0 / CUTOFF) * inv * env)
    s3, s5, s15 = math.sqrt(3.0), math.sqrt(5.0), math.sqrt(15.0)
    ys = (
        s3 * ux,
        s3 * uy,
        s3 * uz,
        s15 * ux * uy,
        s15 * uy * uz,
        0.5 * s5 * (3.0 * uz * uz - 1.0),
        s15 * ux * uz,
        0.5 * s15 * (ux * ux - uy * uy),
    )
    return ys, basis


def silu(z):
    return z * jax.nn.sigmoid(z)


def silu_slope(z):
    sig = jax.nn.sigmoid(z)
    return sig * (1.0 + z * (1.0 - sig))


def invariants_mixed(a, v, q, select):
    n1 = v[0] * v[0] + v[1] * v[1] + v[2] * v[2]
    n2 = q[0] * q[0] + q[1] * q[1] + q[2] * q[2] + q[3] * q[3] + q[4] * q[4]
    rt = 1.0 / math.sqrt(3.0)
    w = (3.0 / math.sqrt(15.0)) * (
        (q[4] - rt * q[2]) * v[0] * v[0]
        + (-q[4] - rt * q[2]) * v[1] * v[1]
        + (2.0 * rt) * q[2] * v[2] * v[2]
        + 2.0 * (q[0] * v[0] * v[1] + q[1] * v[1] * v[2] + q[3] * v[0] * v[2])
    )
    terms = [a, a * a, n1, n2, a * a * a, a * n1, a * n2, w]
    mixed = terms[0] * select[0]
    for p in range(1, 8):
        mixed = mixed + terms[p] * select[p]
    return mixed.astype(BF16)


def node_one(moments, start, select, gates, mix, skip, equi):
    a, v, q = moments[0], moments[1:4], moments[4:9]
    out = mapped(invariants_mixed(a, v, q, select), mix) + mm(start, skip)
    vec_gate = gates[0] + gates[1] * a
    ten_gate = gates[2] + gates[3] * a
    outs = [out]
    outs += [mapped((x * vec_gate).astype(BF16), equi[0]) for x in v]
    outs += [mapped((x * ten_gate).astype(BF16), equi[1]) for x in q]
    return tuple(outs)


def node_two(moments, own, select, mix, skip, readout, head, final):
    own16 = own.astype(BF16)
    mixed = invariants_mixed(moments[0], moments[1:4], moments[4:9], select)
    two = (mapped(mixed, mix) + mapped(own16, skip)).astype(BF16)
    first = jnp.sum(own16.astype(F32) * readout, axis=1, keepdims=True)
    second = jnp.sum(silu(mapped(two, head)) * final, axis=1, keepdims=True)
    return first + second


def two_way(x):
    hi = x.astype(BF16)
    return hi, (x - hi.astype(F32)).astype(BF16)


def spread_matrix(channels):
    rows = lax.broadcasted_iota(jnp.int32, (32, 9 * channels), 0) % 16
    cols = lax.broadcasted_iota(jnp.int32, (32, 9 * channels), 1) // channels
    return (rows == cols).astype(F32).astype(BF16)


def sum_matrix(channels):
    rows = lax.broadcasted_iota(jnp.int32, (16, 8 * channels), 0)
    cols = lax.broadcasted_iota(jnp.int32, (16, 8 * channels), 1) // channels
    return (rows == cols).astype(F32).astype(BF16)


def order_rows(lanes):
    rows = lax.broadcasted_iota(jnp.int32, (8, lanes), 0) + 1
    return rows.astype(F32) * (math.pi / CUTOFF)


def pair_forward(s, slots, live, own, ext_pos, feats, w1t, wht, last, oh, rel, ybuf, zbuf, gbuf, rbuf):
    lanes = slots.shape[2]
    rows = ext_pos.shape[1]
    hot = lax.broadcasted_iota(jnp.int32, (rows, lanes), 0) == slots[s]
    hot = hot.astype(F32).astype(BF16)
    oh[s] = hot
    pos = ext_pos[...]
    hi = pos.astype(BF16)
    rest = pos - hi.astype(F32)
    mid = rest.astype(BF16)
    low = (rest - mid.astype(F32)).astype(BF16)
    r = (mm(hi, hot) + mm(mid, hot)) + mm(low, hot) - own[...]
    rel[s] = r
    ys, basis = geometry(r[0:1], r[1:2], r[2:3], order_rows(lanes))
    alive = live[s]
    ybuf[s] = jnp.zeros_like(ybuf[s])
    ybuf[s, 0:1, :] = alive
    for m in range(8):
        ybuf[s, m + 1 : m + 2, :] = ys[m] * alive
    h = jnp.concatenate([basis, jnp.zeros_like(basis)], axis=0).astype(BF16)
    for layer in range(3):
        z = mm(w1t[...] if layer == 0 else wht[layer - 1], h)
        zbuf[s, layer] = z
        h = silu(z).astype(BF16)
    rbuf[s] = mm(h, last[...], TN).astype(BF16)
    gbuf[s] = mm(hot, feats[...], TN).astype(BF16)


def spread_y(s, ybuf, ye, channels):
    hi, lo = two_way(ybuf[s])
    ye[...] = mm(jnp.concatenate([hi, lo], axis=0), spread_matrix(channels), TN)


def pair_backward(s, dots, live, w1, wh, last, oh, rel, ybuf, zbuf, dr, phi, plo, dposown, dposext):
    lanes = oh.shape[2]
    channels = phi.shape[1] // 8
    ones = sum_matrix(channels)
    dy = mm(ones, phi[...], NT) + mm(ones, plo[...], NT)
    dh = mm(last[...], dr[...], NT).astype(BF16).astype(F32)
    for layer in (2, 1):
        dz = (dh * silu_slope(zbuf[s, layer])).astype(BF16)
        dh = mm(wh[layer - 1], dz).astype(BF16).astype(F32)
    dz = (dh * silu_slope(zbuf[s, 0])).astype(BF16)
    dbasis = mm(w1[...], dz).astype(BF16).astype(F32)[0:8]
    r = rel[s]
    orders = order_rows(lanes)
    _, back = jax.vjp(lambda x, y, z: geometry(x, y, z, orders), r[0:1], r[1:2], r[2:3])
    alive = live[s]
    grads = back((tuple(dy[m : m + 1] * alive for m in range(8)), dbasis))
    r8 = lax.broadcasted_iota(jnp.int32, (8, lanes), 0)
    g = jnp.where(r8 == 0, grads[0], jnp.where(r8 == 1, grads[1], jnp.where(r8 == 2, grads[2], 0.0)))
    hi = g.astype(BF16)
    rest = g - hi.astype(F32)
    mid = rest.astype(BF16)
    low = (rest - mid.astype(F32)).astype(BF16)
    hot = oh[s]
    dposext[...] += mm(hi, hot, NT) + mm(mid, hot, NT) + mm(low, hot, NT)
    width = dposown.shape[1]
    for j in range(lanes // width):
        dposown[...] -= g[:, j * width : (j + 1) * width]


def cut(ref, row, block, channels):
    return ref[row : row + CHUNK, block * channels : (block + 1) * channels]


def accumulate_one(s, atoms, channels, ye, rbuf, gbuf, mom):
    for at in range(0, atoms, CHUNK):
        acc = [mom[m, at : at + CHUNK, :] for m in range(9)]
        for j in range(GROUP):
            row = j * atoms + at
            g = gbuf[s, row : row + CHUNK, :].astype(F32)
            for l in range(3):
                wg = rbuf[s, row : row + CHUNK, l * channels : (l + 1) * channels].astype(F32) * g
                for m in range(l * l, (l + 1) * (l + 1)):
                    acc[m] = acc[m] + cut(ye, row, m, channels) * wg
        for m in range(9):
            mom[m, at : at + CHUNK, :] = acc[m]


def load(ref, s, row, block, channels):
    return ref[s, row : row + CHUNK, block * channels : (block + 1) * channels].astype(F32)


def accumulate_two(s, atoms, channels, ye, rbuf, gbuf, mom):
    for at in range(0, atoms, CHUNK):
        acc = [mom[m, at : at + CHUNK, :] for m in range(9)]
        for j in range(GROUP):
            row = j * atoms + at
            get_r = lambda p: load(rbuf, s, row, p, channels)
            y0 = cut(ye, row, 0, channels)
            g0 = load(gbuf, s, row, 0, channels)
            acc[0] = acc[0] + y0 * get_r(0) * g0
            for first, past, inner, plain, other in ((1, 4, 1, 3, 4), (4, 9, 2, 5, 6)):
                total = None
                pg = get_r(plain) * g0
                po = get_r(other) * y0
                for m in range(first, past):
                    ym = cut(ye, row, m, channels)
                    gm = load(gbuf, s, row, m, channels)
                    total = ym * gm if total is None else total + ym * gm
                    acc[m] = acc[m] + (ym * pg + po * gm)
                acc[0] = acc[0] + get_r(inner) * total
        for m in range(9):
            mom[m, at : at + CHUNK, :] = acc[m]


def put_product(phi, plo, row, m, channels, value):
    hi, lo = two_way(value)
    phi[row : row + CHUNK, (m - 1) * channels : m * channels] = hi
    plo[row : row + CHUNK, (m - 1) * channels : m * channels] = lo


def differentiate_one(s, atoms, channels, ye, rbuf, gbuf, dmom, dr, phi, plo):
    for at in range(0, atoms, CHUNK):
        dm = [dmom[m, at : at + CHUNK, :] for m in range(9)]
        for j in range(GROUP):
            row = j * atoms + at
            g = gbuf[s, row : row + CHUNK, :].astype(F32)
            for l in range(3):
                wg = load(rbuf, s, row, l, channels) * g if l else None
                total = None
                for m in range(l * l, (l + 1) * (l + 1)):
                    t = cut(ye, row, m, channels) * dm[m]
                    total = t if total is None else total + t
                    if l:
                        put_product(phi, plo, row, m, channels, wg * dm[m])
                dr[row : row + CHUNK, l * channels : (l + 1) * channels] = (total * g).astype(BF16)


def differentiate_two(s, atoms, channels, ye, rbuf, gbuf, dmom, dr, phi, plo, dgh, dgl):
    for at in range(0, atoms, CHUNK):
        dm = [dmom[m, at : at + CHUNK, :] for m in range(9)]
        for j in range(GROUP):
            row = j * atoms + at

            def put_r(p, value):
                dr[row : row + CHUNK, p * channels : (p + 1) * channels] = value.astype(BF16)

            def put_g(m, value):
                hi, lo = two_way(value)
                dgh[row : row + CHUNK, m * channels : (m + 1) * channels] = hi
                dgl[row : row + CHUNK, m * channels : (m + 1) * channels] = lo

            y0 = cut(ye, row, 0, channels)
            g0 = load(gbuf, s, row, 0, channels)
            da = dm[0]
            y0da = y0 * da
            put_r(0, y0da * g0)
            dg0 = y0da * load(rbuf, s, row, 0, channels)
            for first, past, inner, plain, other in ((1, 4, 1, 3, 4), (4, 9, 2, 5, 6)):
                rp = load(rbuf, s, row, plain, channels)
                ai = load(rbuf, s, row, inner, channels) * da
                bp = rp * g0
                po = load(rbuf, s, row, other, channels) * y0
                big_s = big_d = big_e = None
                for m in range(first, past):
                    ym = cut(ye, row, m, channels)
                    gm = load(gbuf, s, row, m, channels)
                    t1, t2, t3 = ym * gm, ym * dm[m], gm * dm[m]
                    big_s = t1 if big_s is None else big_s + t1
                    big_d = t2 if big_d is None else big_d + t2
                    big_e = t3 if big_e is None else big_e + t3
                    put_g(m, ym * ai + po * dm[m])
                    put_product(phi, plo, row, m, channels, ai * gm + bp * dm[m])
                put_r(inner, big_s * da)
                put_r(plain, g0 * big_d)
                put_r(other, y0 * big_e)
                dg0 = dg0 + rp * big_d
            put_g(0, dg0)


def columns(ref, count, channels):
    return [ref[:, p * channels : (p + 1) * channels].astype(F32) for p in range(count)]


def first_forward(
    steps, slots, live, own, ext_pos, start, w1t, wht, last, select, gates, mix, skip, equi, pick,
    mom, out, packets, oh, rel, ybuf, zbuf, gbuf, rbuf, ye,
):
    atoms, channels = mom.shape[1:]
    mom[...] = jnp.zeros_like(mom)

    @pl.loop(0, steps)
    def _(s):
        pair_forward(s, slots, live, own, ext_pos, start, w1t, wht, last, oh, rel, ybuf, zbuf, gbuf, rbuf)
        spread_y(s, ybuf, ye, channels)
        accumulate_one(s, atoms, channels, ye, rbuf, gbuf, mom)

    outs = node_one(
        tuple(mom[m] for m in range(9)), start[0:atoms, :], columns(select, 8, channels),
        columns(gates, 4, channels), mix[...], skip[...], (equi[0], equi[1]),
    )
    for m in range(9):
        out[:, m * channels : (m + 1) * channels] = outs[m].astype(BF16)
    packets[...] = mm(pick[...], out[...]).astype(BF16)


def second_both(
    steps, slots, live, own, ext_pos, feats, w1t, w1, wht, wh, last, select, mix, skip, readout, head, final,
    energy, gown, gpackets, dposown, dposext,
    oh, rel, ybuf, zbuf, gbuf, rbuf, ye, mom, dr, phi, plo, dgh, dgl, gext,
):
    atoms, channels = mom.shape[1:]
    mom[...] = jnp.zeros_like(mom)

    @pl.loop(0, steps)
    def _(s):
        pair_forward(s, slots, live, own, ext_pos, feats, w1t, wht, last, oh, rel, ybuf, zbuf, gbuf, rbuf)
        spread_y(s, ybuf, ye, channels)
        accumulate_two(s, atoms, channels, ye, rbuf, gbuf, mom)

    sel = columns(select, 8, channels)

    def node(moments, own_feat):
        return node_two(moments, own_feat, sel, mix[...], skip[...], readout[...], head[...], final[...])

    value, back = jax.vjp(node, tuple(mom[m] for m in range(9)), feats[0:atoms, 0:channels].astype(F32))
    energy[...] = value
    dmoms, down = back(jnp.ones_like(value))
    for m in range(9):
        mom[m] = dmoms[m]
    gext[...] = jnp.zeros_like(gext)
    gext[0:atoms, 0:channels] = down
    dposown[...] = jnp.zeros_like(dposown)
    dposext[...] = jnp.zeros_like(dposext)

    @pl.loop(0, steps)
    def _(s):
        spread_y(s, ybuf, ye, channels)
        differentiate_two(s, atoms, channels, ye, rbuf, gbuf, mom, dr, phi, plo, dgh, dgl)
        gext[...] += mm(oh[s], dgh[...]) + mm(oh[s], dgl[...])
        pair_backward(s, None, live, w1, wh, last, oh, rel, ybuf, zbuf, dr, phi, plo, dposown, dposext)

    gown[...] = gext[0:atoms, :]
    gpackets[...] = gext[atoms:, :].astype(BF16)


def first_backward(
    steps, slots, live, own, ext_pos, start, w1t, w1, wht, wh, last, select, gates, mix, skip, equi, pick,
    mom, gown, returned, posown0, posext0,
    dposown, dposext,
    oh, rel, ybuf, zbuf, gbuf, rbuf, ye, dmom, dr, phi, plo,
):
    atoms, channels = mom.shape[1:]
    total = (gown[...] + mm(pick[...], returned[...], TN)).astype(BF16).astype(F32)
    sel, gat = columns(select, 8, channels), columns(gates, 4, channels)

    def node(moments):
        return node_one(moments, start[0:atoms, :], sel, gat, mix[...], skip[...], (equi[0], equi[1]))

    _, back = jax.vjp(node, tuple(mom[m] for m in range(9)))
    cts = tuple(total[:, m * channels : (m + 1) * channels] for m in range(9))
    (dmoms,) = back(cts)
    for m in range(9):
        dmom[m] = dmoms[m]
    dposown[...] = posown0[...]
    dposext[...] = posext0[...]

    @pl.loop(0, steps)
    def _(s):
        pair_forward(s, slots, live, own, ext_pos, start, w1t, wht, last, oh, rel, ybuf, zbuf, gbuf, rbuf)
        spread_y(s, ybuf, ye, channels)
        differentiate_one(s, atoms, channels, ye, rbuf, gbuf, dmom, dr, phi, plo)
        pair_backward(s, None, live, w1, wh, last, oh, rel, ybuf, zbuf, dr, phi, plo, dposown, dposext)


def swap_kernel(n_slab, n_brick, face, sign, src, dst, send, recv):
    slab, brick = lax.axis_index("slab"), lax.axis_index("brick")

    def there(d, way):
        ds, db = DIRECTIONS[d]
        return (
            lax.rem(slab + way * ds + n_slab, n_slab),
            lax.rem(brick + way * db + n_brick, n_brick),
        )

    barrier = pltpu.get_barrier_semaphore()
    for d in range(8):
        pl.semaphore_signal(barrier, inc=1, device_id=there(d, 1), device_id_type=MESH)
    pl.semaphore_wait(barrier, 8)
    copies = []
    for d in range(8):
        rows = pl.ds(d * face, face) if d < 4 else pl.ds(4 * face + (d - 4) * EDGE, EDGE)
        copy = pltpu.make_async_remote_copy(
            src_ref=src.at[rows], dst_ref=dst.at[rows], send_sem=send.at[d], recv_sem=recv.at[d],
            device_id=there(d, sign), device_id_type=MESH,
        )
        copy.start()
        copies.append(copy)
    for copy in copies:
        copy.wait()


VM = pl.BlockSpec(memory_space=pltpu.VMEM)


def swap(packets, sign, face, number):
    return pl.pallas_call(
        functools.partial(swap_kernel, lax.axis_size("slab"), lax.axis_size("brick"), face, sign),
        out_shape=jax.ShapeDtypeStruct(packets.shape, packets.dtype),
        in_specs=[VM],
        out_specs=VM,
        scratch_shapes=[pltpu.SemaphoreType.DMA((8,)), pltpu.SemaphoreType.DMA((8,))],
        compiler_params=pltpu.CompilerParams(collective_id=number, has_side_effects=True),
        name="swap" + str(number),
    )(packets)


def call(kernel, name, args, outs, scratch):
    return pl.pallas_call(
        kernel,
        out_shape=outs,
        in_specs=[VM] * len(args),
        out_specs=[VM] * len(outs),
        scratch_shapes=scratch,
        compiler_params=pltpu.CompilerParams(vmem_limit_bytes=58 * 1024 * 1024),
        name=name,
    )(*args)


def shards(
    positions, species, neighbour_slot, neighbour_count, face_rows, edge_rows, embedding, radial_first,
    radial_hidden, radial_last_one, radial_last_two, product_weight, mix_weight, skip_weight, equi_weight,
    equi_mix, atom_reference, readout_weight, head_weight, final_weight,
):
    atoms, slot_count = neighbour_slot.shape
    face, edge = face_rows.shape[2], edge_rows.shape[2]
    channels = embedding.shape[1]
    kinds_n = embedding.shape[0]
    steps, lanes = slot_count // GROUP, GROUP * atoms
    ghosts = 4 * face + 4 * EDGE
    rows = atoms + ghosts
    span = LXZ * SPACING
    first_edge = atoms + 4 * face

    kinds = jnp.arange(kinds_n, dtype=jnp.int32)
    onehot = (species[:, None] == kinds[None, :]).astype(BF16)
    table = jnp.concatenate(
        [
            face_rows[0].reshape(-1),
            jnp.pad(edge_rows[0], ((0, 0), (0, EDGE - edge)), constant_values=-1).reshape(-1),
        ]
    )
    pick_mask = table[:, None] == jnp.arange(atoms, dtype=jnp.int32)[None, :]
    pick = pick_mask.astype(BF16)

    carried = jnp.concatenate([positions, species.astype(F32)[None], jnp.zeros((channels - 4, atoms), F32)], axis=0)
    packet = lax.dot_general(
        pick_mask.astype(F32), carried, (((1,), (1,)), ((), ())), precision=lax.Precision.HIGHEST,
        preferred_element_type=F32,
    )
    arrived = swap(packet, -1, face, 0)[:, :8]
    moves = []
    for d in range(8):
        ds, db = DIRECTIONS[d]
        moves += [(db * span, 0.0, ds * span)] * (face if d < 4 else EDGE)
    ghost_pos = arrived[:, :3] + jnp.array(moves, F32)
    ghost_hot = (arrived[:, 3:4] == kinds.astype(F32)[None, :]).astype(BF16)
    ext_start = jnp.dot(
        jnp.concatenate([onehot, ghost_hot], axis=0), embedding, preferred_element_type=F32
    ).astype(BF16)
    ext_pos = jnp.pad(jnp.concatenate([positions, ghost_pos.T], axis=1), ((0, 5), (0, 0)))
    own = jnp.tile(jnp.pad(positions, ((0, 5), (0, 0))), (1, GROUP))

    past = neighbour_slot - first_edge
    slots = jnp.where(past >= 0, first_edge + (past // edge) * EDGE + past % edge, neighbour_slot)
    slots = slots.T.reshape(steps, 1, lanes)
    live = (jnp.arange(slot_count)[:, None] < neighbour_count[None, :]).astype(F32)
    live = (live / math.sqrt(slot_count)).reshape(steps, 1, lanes)

    select_one = jnp.dot(onehot, product_weight[0], preferred_element_type=F32)
    select_two = jnp.dot(onehot, product_weight[1], preferred_element_type=F32)
    gates = jnp.dot(onehot, equi_weight, preferred_element_type=F32)
    w1 = jnp.pad(radial_first, ((0, 0), (0, 8), (0, 0)))
    w1t = w1.transpose(0, 2, 1)
    wht = radial_hidden.transpose(0, 1, 3, 2)
    rad = radial_hidden.shape[-1]

    def struct(shape, dtype):
        return jax.ShapeDtypeStruct(shape, dtype)

    def common(feature_width, paths):
        return [
            pltpu.VMEM((steps, rows, lanes), BF16),
            pltpu.VMEM((steps, 8, lanes), F32),
            pltpu.VMEM((steps, 16, lanes), F32),
            pltpu.VMEM((steps, 3, rad, lanes), F32),
            pltpu.VMEM((steps, lanes, feature_width), BF16),
            pltpu.VMEM((steps, lanes, paths * channels), BF16),
            pltpu.VMEM((lanes, 9 * channels), F32),
        ]

    mom, layer_one, packets = call(
        functools.partial(first_forward, steps),
        "layer_one_forward",
        (slots, live, own, ext_pos, ext_start, w1t[0], wht[0], radial_last_one, select_one, gates,
         mix_weight[0], skip_weight[0], equi_mix, pick),
        [struct((9, atoms, channels), F32), struct((atoms, 9 * channels), BF16), struct((ghosts, 9 * channels), BF16)],
        common(channels, 3),
    )
    ext_one = jnp.concatenate([layer_one, swap(packets, -1, face, 1)], axis=0)
    moment_scratch = pltpu.VMEM((9, atoms, channels), F32)
    energy, gown, gpackets, posown, posext = call(
        functools.partial(second_both, steps),
        "layer_two",
        (slots, live, own, ext_pos, ext_one, w1t[1], w1[1], wht[1], radial_hidden[1], radial_last_two, select_two,
         mix_weight[1], skip_weight[1], readout_weight.astype(F32)[None], head_weight, final_weight.astype(F32)[None]),
        [struct((atoms, 1), F32), struct((atoms, 9 * channels), F32), struct((ghosts, 9 * channels), BF16),
         struct((8, atoms), F32), struct((8, rows), F32)],
        common(9 * channels, 7)
        + [moment_scratch, pltpu.VMEM((lanes, 7 * channels), BF16)]
        + [pltpu.VMEM((lanes, 8 * channels), BF16)] * 2
        + [pltpu.VMEM((lanes, 9 * channels), BF16)] * 2
        + [pltpu.VMEM((rows, 9 * channels), F32)],
    )
    returned = swap(gpackets, 1, face, 2)
    posown, posext = call(
        functools.partial(first_backward, steps),
        "layer_one_backward",
        (slots, live, own, ext_pos, ext_start, w1t[0], w1[0], wht[0], radial_hidden[0], radial_last_one, select_one,
         gates, mix_weight[0], skip_weight[0], equi_mix, pick, mom, gown, returned, posown, posext),
        [struct((8, atoms), F32), struct((8, rows), F32)],
        common(channels, 3)
        + [moment_scratch, pltpu.VMEM((lanes, 3 * channels), BF16)]
        + [pltpu.VMEM((lanes, 8 * channels), BF16)] * 2,
    )
    back = jnp.pad(posext[:, atoms:].T, ((0, 0), (0, channels - 8)))
    back = swap(back, 1, face, 3)[:, :8]
    gathered = lax.dot_general(
        back, pick_mask.astype(F32), TN, precision=lax.Precision.HIGHEST, preferred_element_type=F32
    )
    total = posown + posext[:, :atoms] + gathered
    base = jnp.sum(jnp.where(species[:, None] == kinds[None, :], atom_reference[None, :], 0.0), axis=1)
    return (base + energy[:, 0], -total[:3])


def solution(mesh):
    every = ("slab", "brick")
    placed = (P(None, every), P(every), P(every, None), P(every), P(every, None, None), P(every, None, None))
    placed = placed + (P(),) * 14
    return jax.shard_map(
        shards, mesh=mesh, in_specs=placed, out_specs=(P(every), P(None, every)), check_vma=False
    )
```

```python
import functools
import math

import jax
import jax.numpy as jnp
from jax import lax
from jax.experimental import pallas as pl
from jax.experimental.pallas import tpu as pltpu
from jax.sharding import PartitionSpec as P

LXZ = 4
SPACING = 2.2
CUTOFF = 6.0
DIRECTIONS = ((0, 1), (0, -1), (1, 0), (-1, 0), (1, 1), (1, -1), (-1, 1), (-1, -1))
MESH = pl.DeviceIdType.MESH
F32 = jnp.float32
BF16 = jnp.bfloat16
GROUP = 4
EDGE = 16
CHUNK = 16
NN = (((1,), (0,)), ((), ()))
NT = (((1,), (1,)), ((), ()))
TN = (((0,), (0,)), ((), ()))


def mm(a, b, dims=NN):
    return lax.dot_general(a, b, dims, preferred_element_type=F32)


@jax.custom_vjp
def mapped(x, weight):
    return mm(x, weight)


def mapped_fwd(x, weight):
    return mm(x, weight), weight


def mapped_bwd(weight, ct):
    hi, lo = two_way(ct)
    return (mm(hi, weight, NT) + mm(lo, weight, NT)).astype(BF16), jnp.zeros_like(weight)


mapped.defvjp(mapped_fwd, mapped_bwd)


def geometry(rx, ry, rz, orders):
    dist = jnp.sqrt(rx * rx + ry * ry + rz * rz)
    inv = 1.0 / dist
    ux, uy, uz = rx * inv, ry * inv, rz * inv
    x = dist * (1.0 / CUTOFF)
    x2 = x * x
    x5 = x2 * x2 * x
    env = 1.0 - 21.0 * x5 + 35.0 * x5 * x - 15.0 * x5 * x2
    basis = jnp.sin(dist * orders) * (math.sqrt(2.0 / CUTOFF) * inv * env)
    s3, s5, s15 = math.sqrt(3.0), math.sqrt(5.0), math.sqrt(15.0)
    ys = (
        s3 * ux,
        s3 * uy,
        s3 * uz,
        s15 * ux * uy,
        s15 * uy * uz,
        0.5 * s5 * (3.0 * uz * uz - 1.0),
        s15 * ux * uz,
        0.5 * s15 * (ux * ux - uy * uy),
    )
    return ys, basis


def silu(z):
    return z * jax.nn.sigmoid(z)


def silu_slope(z):
    sig = jax.nn.sigmoid(z)
    return sig * (1.0 + z * (1.0 - sig))


def invariants_mixed(a, v, q, select):
    n1 = v[0] * v[0] + v[1] * v[1] + v[2] * v[2]
    n2 = q[0] * q[0] + q[1] * q[1] + q[2] * q[2] + q[3] * q[3] + q[4] * q[4]
    rt = 1.0 / math.sqrt(3.0)
    w = (3.0 / math.sqrt(15.0)) * (
        (q[4] - rt * q[2]) * v[0] * v[0]
        + (-q[4] - rt * q[2]) * v[1] * v[1]
        + (2.0 * rt) * q[2] * v[2] * v[2]
        + 2.0 * (q[0] * v[0] * v[1] + q[1] * v[1] * v[2] + q[3] * v[0] * v[2])
    )
    terms = [a, a * a, n1, n2, a * a * a, a * n1, a * n2, w]
    mixed = terms[0] * select[0]
    for p in range(1, 8):
        mixed = mixed + terms[p] * select[p]
    return mixed.astype(BF16)


def node_one(moments, start, select, gates, mix, skip, equi):
    a, v, q = moments[0], moments[1:4], moments[4:9]
    out = mapped(invariants_mixed(a, v, q, select), mix) + mm(start, skip)
    vec_gate = gates[0] + gates[1] * a
    ten_gate = gates[2] + gates[3] * a
    outs = [out]
    outs += [mapped((x * vec_gate).astype(BF16), equi[0]) for x in v]
    outs += [mapped((x * ten_gate).astype(BF16), equi[1]) for x in q]
    return tuple(outs)


def node_two(moments, own, select, mix, skip, readout, head, final):
    own16 = own.astype(BF16)
    mixed = invariants_mixed(moments[0], moments[1:4], moments[4:9], select)
    two = (mapped(mixed, mix) + mapped(own16, skip)).astype(BF16)
    first = jnp.sum(own16.astype(F32) * readout, axis=1, keepdims=True)
    second = jnp.sum(silu(mapped(two, head)) * final, axis=1, keepdims=True)
    return first + second


def two_way(x):
    hi = x.astype(BF16)
    return hi, (x - hi.astype(F32)).astype(BF16)


def spread_matrix(channels):
    rows = lax.broadcasted_iota(jnp.int32, (32, 9 * channels), 0) % 16
    cols = lax.broadcasted_iota(jnp.int32, (32, 9 * channels), 1) // channels
    return (rows == cols).astype(F32).astype(BF16)


def sum_matrix(channels):
    rows = lax.broadcasted_iota(jnp.int32, (16, 8 * channels), 0)
    cols = lax.broadcasted_iota(jnp.int32, (16, 8 * channels), 1) // channels
    return (rows == cols).astype(F32).astype(BF16)


def order_rows(lanes):
    rows = lax.broadcasted_iota(jnp.int32, (8, lanes), 0) + 1
    return rows.astype(F32) * (math.pi / CUTOFF)


def pair_forward(s, slots, live, own, ext_pos, feats, w1t, wht, last, oh, rel, ybuf, zbuf, gbuf, rbuf):
    lanes = slots.shape[2]
    rows = ext_pos.shape[1]
    hot = lax.broadcasted_iota(jnp.int32, (rows, lanes), 0) == slots[s]
    hot = hot.astype(F32).astype(BF16)
    oh[s] = hot
    pos = ext_pos[...]
    hi = pos.astype(BF16)
    rest = pos - hi.astype(F32)
    mid = rest.astype(BF16)
    low = (rest - mid.astype(F32)).astype(BF16)
    r = (mm(hi, hot) + mm(mid, hot)) + mm(low, hot) - own[...]
    rel[s] = r
    ys, basis = geometry(r[0:1], r[1:2], r[2:3], order_rows(lanes))
    alive = live[s]
    ybuf[s] = jnp.zeros_like(ybuf[s])
    ybuf[s, 0:1, :] = alive
    for m in range(8):
        ybuf[s, m + 1 : m + 2, :] = ys[m] * alive
    h = jnp.concatenate([basis, jnp.zeros_like(basis)], axis=0).astype(BF16)
    for layer in range(3):
        z = mm(w1t[...] if layer == 0 else wht[layer - 1], h)
        zbuf[s, layer] = z
        h = silu(z).astype(BF16)
    rbuf[s] = mm(h, last[...], TN).astype(BF16)
    gbuf[s] = mm(hot, feats[...], TN).astype(BF16)


def spread_y(s, ybuf, ye, channels):
    hi, lo = two_way(ybuf[s])
    ye[...] = mm(jnp.concatenate([hi, lo], axis=0), spread_matrix(channels), TN)


def pair_backward(s, hot, live, w1, wh, last, rel, ybuf, zbuf, dr, phi, plo, dposown, dposext):
    lanes = hot.shape[1]
    channels = phi.shape[1] // 8
    ones = sum_matrix(channels)
    dy = mm(ones, phi[...], NT) + mm(ones, plo[...], NT)
    dh = mm(last[...], dr[...], NT).astype(BF16).astype(F32)
    for layer in (2, 1):
        hi, lo = two_way(dh * silu_slope(zbuf[s, layer]))
        dh = (mm(wh[layer - 1], hi) + mm(wh[layer - 1], lo)).astype(BF16).astype(F32)
    hi, lo = two_way(dh * silu_slope(zbuf[s, 0]))
    dbasis = (mm(w1[...], hi) + mm(w1[...], lo)).astype(BF16).astype(F32)[0:8]
    r = rel[s]
    orders = order_rows(lanes)
    _, back = jax.vjp(lambda x, y, z: geometry(x, y, z, orders), r[0:1], r[1:2], r[2:3])
    alive = live[s]
    grads = back((tuple(dy[m : m + 1] * alive for m in range(8)), dbasis))
    r8 = lax.broadcasted_iota(jnp.int32, (8, lanes), 0)
    g = jnp.where(r8 == 0, grads[0], jnp.where(r8 == 1, grads[1], jnp.where(r8 == 2, grads[2], 0.0)))
    hi = g.astype(BF16)
    rest = g - hi.astype(F32)
    mid = rest.astype(BF16)
    low = (rest - mid.astype(F32)).astype(BF16)
    dposext[...] += mm(hi, hot, NT) + mm(mid, hot, NT) + mm(low, hot, NT)
    width = dposown.shape[1]
    for j in range(lanes // width):
        dposown[...] -= g[:, j * width : (j + 1) * width]


def cut(ref, row, block, channels):
    return ref[row : row + CHUNK, block * channels : (block + 1) * channels]


def accumulate_one(s, atoms, channels, ye, rbuf, gbuf, mom):
    for at in range(0, atoms, CHUNK):
        acc = [mom[m, at : at + CHUNK, :] for m in range(9)]
        for j in range(GROUP):
            row = j * atoms + at
            g = gbuf[s, row : row + CHUNK, :].astype(F32)
            for l in range(3):
                wg = rbuf[s, row : row + CHUNK, l * channels : (l + 1) * channels].astype(F32) * g
                for m in range(l * l, (l + 1) * (l + 1)):
                    acc[m] = acc[m] + cut(ye, row, m, channels) * wg
        for m in range(9):
            mom[m, at : at + CHUNK, :] = acc[m]


def load(ref, s, row, block, channels):
    return ref[s, row : row + CHUNK, block * channels : (block + 1) * channels].astype(F32)


def accumulate_two(s, atoms, channels, ye, rbuf, gbuf, mom):
    for at in range(0, atoms, CHUNK):
        acc = [mom[m, at : at + CHUNK, :] for m in range(9)]
        for j in range(GROUP):
            row = j * atoms + at
            get_r = lambda p: load(rbuf, s, row, p, channels)
            y0 = cut(ye, row, 0, channels)
            g0 = load(gbuf, s, row, 0, channels)
            acc[0] = acc[0] + y0 * get_r(0) * g0
            for first, past, inner, plain, other in ((1, 4, 1, 3, 4), (4, 9, 2, 5, 6)):
                total = None
                pg = get_r(plain) * g0
                po = get_r(other) * y0
                for m in range(first, past):
                    ym = cut(ye, row, m, channels)
                    gm = load(gbuf, s, row, m, channels)
                    total = ym * gm if total is None else total + ym * gm
                    acc[m] = acc[m] + (ym * pg + po * gm)
                acc[0] = acc[0] + get_r(inner) * total
        for m in range(9):
            mom[m, at : at + CHUNK, :] = acc[m]


def put_product(phi, plo, row, m, channels, value):
    hi, lo = two_way(value)
    phi[row : row + CHUNK, (m - 1) * channels : m * channels] = hi
    plo[row : row + CHUNK, (m - 1) * channels : m * channels] = lo


def differentiate_one(s, atoms, channels, ye, rbuf, gbuf, dmom, dr, phi, plo):
    for at in range(0, atoms, CHUNK):
        dm = [dmom[m, at : at + CHUNK, :] for m in range(9)]
        for j in range(GROUP):
            row = j * atoms + at
            g = gbuf[s, row : row + CHUNK, :].astype(F32)
            for l in range(3):
                wg = load(rbuf, s, row, l, channels) * g if l else None
                total = None
                for m in range(l * l, (l + 1) * (l + 1)):
                    t = cut(ye, row, m, channels) * dm[m]
                    total = t if total is None else total + t
                    if l:
                        put_product(phi, plo, row, m, channels, wg * dm[m])
                dr[row : row + CHUNK, l * channels : (l + 1) * channels] = (total * g).astype(BF16)


def differentiate_two(s, atoms, channels, ye, rbuf, gbuf, dmom, dr, phi, plo, dgh):
    for at in range(0, atoms, CHUNK):
        dm = [dmom[m, at : at + CHUNK, :] for m in range(9)]
        for j in range(GROUP):
            row = j * atoms + at

            def put_r(p, value):
                dr[row : row + CHUNK, p * channels : (p + 1) * channels] = value.astype(BF16)

            def put_g(m, value):
                dgh[row : row + CHUNK, m * channels : (m + 1) * channels] = value.astype(BF16)

            y0 = cut(ye, row, 0, channels)
            g0 = load(gbuf, s, row, 0, channels)
            da = dm[0]
            y0da = y0 * da
            put_r(0, y0da * g0)
            dg0 = y0da * load(rbuf, s, row, 0, channels)
            for first, past, inner, plain, other in ((1, 4, 1, 3, 4), (4, 9, 2, 5, 6)):
                rp = load(rbuf, s, row, plain, channels)
                ai = load(rbuf, s, row, inner, channels) * da
                bp = rp * g0
                po = load(rbuf, s, row, other, channels) * y0
                big_s = big_d = big_e = None
                for m in range(first, past):
                    ym = cut(ye, row, m, channels)
                    gm = load(gbuf, s, row, m, channels)
                    t1, t2, t3 = ym * gm, ym * dm[m], gm * dm[m]
                    big_s = t1 if big_s is None else big_s + t1
                    big_d = t2 if big_d is None else big_d + t2
                    big_e = t3 if big_e is None else big_e + t3
                    put_g(m, ym * ai + po * dm[m])
                    put_product(phi, plo, row, m, channels, ai * gm + bp * dm[m])
                put_r(inner, big_s * da)
                put_r(plain, g0 * big_d)
                put_r(other, y0 * big_e)
                dg0 = dg0 + rp * big_d
            put_g(0, dg0)


def columns(ref, count, channels):
    return [ref[:, p * channels : (p + 1) * channels].astype(F32) for p in range(count)]


def first_forward(
    steps, slots, live, own, ext_pos, start, w1t, wht, last, select, gates, mix, skip, equi, pick,
    mom, out, packets, rel, ybuf, zbuf, gbuf, rbuf, oh, ye,
):
    atoms, channels = mom.shape[1:]
    mom[...] = jnp.zeros_like(mom)

    @pl.loop(0, steps, unroll=2)
    def _(s):
        pair_forward(s, slots, live, own, ext_pos, start, w1t, wht, last, oh, rel, ybuf, zbuf, gbuf, rbuf)
        spread_y(s, ybuf, ye, channels)
        accumulate_one(s, atoms, channels, ye, rbuf, gbuf, mom)

    outs = node_one(
        tuple(mom[m] for m in range(9)), start[0:atoms, :], columns(select, 8, channels),
        columns(gates, 4, channels), mix[...], skip[...], (equi[0], equi[1]),
    )
    for m in range(9):
        out[:, m * channels : (m + 1) * channels] = outs[m].astype(BF16)
    packets[...] = mm(pick[...], out[...]).astype(BF16)


def second_both(
    steps, slots, live, own, ext_pos, mine, ghost, w1t, w1, wht, wh, last, select, mix, skip, readout, head, final,
    energy, gown, gpackets, dposown, dposext,
    oh, rel, ybuf, zbuf, gbuf, rbuf, ye, mom, dr, phi, plo, dgh, feats, gext,
):
    atoms, channels = mom.shape[1:]
    feats[0:atoms, :] = mine[...]
    feats[atoms:, :] = ghost[...]
    mom[...] = jnp.zeros_like(mom)

    @pl.loop(0, steps, unroll=2)
    def _(s):
        pair_forward(s, slots, live, own, ext_pos, feats, w1t, wht, last, oh, rel, ybuf, zbuf, gbuf, rbuf)
        spread_y(s, ybuf, ye, channels)
        accumulate_two(s, atoms, channels, ye, rbuf, gbuf, mom)

    sel = columns(select, 8, channels)

    def node(moments, own_feat):
        return node_two(moments, own_feat, sel, mix[...], skip[...], readout[...], head[...], final[...])

    value, back = jax.vjp(node, tuple(mom[m] for m in range(9)), feats[0:atoms, 0:channels].astype(F32))
    energy[...] = value
    dmoms, down = back(jnp.ones_like(value))
    for m in range(9):
        mom[m] = dmoms[m]
    gext[...] = jnp.zeros_like(gext)
    gext[0:atoms, 0:channels] = down
    dposown[...] = jnp.zeros_like(dposown)
    dposext[...] = jnp.zeros_like(dposext)

    @pl.loop(0, steps, unroll=2)
    def _(s):
        spread_y(s, ybuf, ye, channels)
        differentiate_two(s, atoms, channels, ye, rbuf, gbuf, mom, dr, phi, plo, dgh)
        gext[...] += mm(oh[s], dgh[...])
        pair_backward(s, oh[s], live, w1, wh, last, rel, ybuf, zbuf, dr, phi, plo, dposown, dposext)

    gown[...] = gext[0:atoms, :]
    gpackets[...] = gext[atoms:, :].astype(BF16)


def first_backward(
    steps, slots, live, start, w1, wh, last, select, gates, mix, skip, equi, pick,
    mom, gown, returned, posown0, posext0, rel, ybuf, zbuf, gbuf, rbuf,
    dposown, dposext,
    oh, ye, dmom, dr, phi, plo,
):
    atoms, channels = mom.shape[1:]
    total = (gown[...] + mm(pick[...], returned[...], TN)).astype(BF16).astype(F32)
    sel, gat = columns(select, 8, channels), columns(gates, 4, channels)

    def node(moments):
        return node_one(moments, start[0:atoms, :], sel, gat, mix[...], skip[...], (equi[0], equi[1]))

    _, back = jax.vjp(node, tuple(mom[m] for m in range(9)))
    cts = tuple(total[:, m * channels : (m + 1) * channels] for m in range(9))
    (dmoms,) = back(cts)
    for m in range(9):
        dmom[m] = dmoms[m]
    dposown[...] = posown0[...]
    dposext[...] = posext0[...]

    @pl.loop(0, steps, unroll=2)
    def _(s):
        hot = lax.broadcasted_iota(jnp.int32, oh.shape, 0) == slots[s]
        oh[...] = hot.astype(F32).astype(BF16)
        spread_y(s, ybuf, ye, channels)
        differentiate_one(s, atoms, channels, ye, rbuf, gbuf, dmom, dr, phi, plo)
        pair_backward(s, oh[...], live, w1, wh, last, rel, ybuf, zbuf, dr, phi, plo, dposown, dposext)


def swap_kernel(n_slab, n_brick, face, sign, src, dst, send, recv):
    slab, brick = lax.axis_index("slab"), lax.axis_index("brick")

    def there(d, way):
        ds, db = DIRECTIONS[d]
        return (
            lax.rem(slab + way * ds + n_slab, n_slab),
            lax.rem(brick + way * db + n_brick, n_brick),
        )

    barrier = pltpu.get_barrier_semaphore()
    for d in range(8):
        pl.semaphore_signal(barrier, inc=1, device_id=there(d, 1), device_id_type=MESH)
    pl.semaphore_wait(barrier, 8)
    copies = []
    for d in range(8):
        rows = pl.ds(d * face, face) if d < 4 else pl.ds(4 * face + (d - 4) * EDGE, EDGE)
        copy = pltpu.make_async_remote_copy(
            src_ref=src.at[rows], dst_ref=dst.at[rows], send_sem=send.at[d], recv_sem=recv.at[d],
            device_id=there(d, sign), device_id_type=MESH,
        )
        copy.start()
        copies.append(copy)
    for copy in copies:
        copy.wait()


VM = pl.BlockSpec(memory_space=pltpu.VMEM)


def swap(packets, sign, face, number):
    return pl.pallas_call(
        functools.partial(swap_kernel, lax.axis_size("slab"), lax.axis_size("brick"), face, sign),
        out_shape=jax.ShapeDtypeStruct(packets.shape, packets.dtype),
        in_specs=[VM],
        out_specs=VM,
        scratch_shapes=[pltpu.SemaphoreType.DMA((8,)), pltpu.SemaphoreType.DMA((8,))],
        compiler_params=pltpu.CompilerParams(collective_id=number, has_side_effects=True),
        name="swap" + str(number),
    )(packets)


def call(kernel, name, args, outs, scratch):
    return pl.pallas_call(
        kernel,
        out_shape=outs,
        in_specs=[VM] * len(args),
        out_specs=[VM] * len(outs),
        scratch_shapes=scratch,
        compiler_params=pltpu.CompilerParams(vmem_limit_bytes=58 * 1024 * 1024),
        name=name,
    )(*args)


def shards(
    positions, species, neighbour_slot, neighbour_count, face_rows, edge_rows, embedding, radial_first,
    radial_hidden, radial_last_one, radial_last_two, product_weight, mix_weight, skip_weight, equi_weight,
    equi_mix, atom_reference, readout_weight, head_weight, final_weight,
):
    atoms, slot_count = neighbour_slot.shape
    face, edge = face_rows.shape[2], edge_rows.shape[2]
    channels = embedding.shape[1]
    kinds_n = embedding.shape[0]
    steps, lanes = slot_count // GROUP, GROUP * atoms
    ghosts = 4 * face + 4 * EDGE
    rows = atoms + ghosts
    span = LXZ * SPACING
    first_edge = atoms + 4 * face

    kinds = jnp.arange(kinds_n, dtype=jnp.int32)
    onehot = (species[:, None] == kinds[None, :]).astype(BF16)
    table = jnp.concatenate(
        [
            face_rows[0].reshape(-1),
            jnp.pad(edge_rows[0], ((0, 0), (0, EDGE - edge)), constant_values=-1).reshape(-1),
        ]
    )
    pick_mask = table[:, None] == jnp.arange(atoms, dtype=jnp.int32)[None, :]
    pick = pick_mask.astype(BF16)

    carried = jnp.concatenate([positions, species.astype(F32)[None], jnp.zeros((channels - 4, atoms), F32)], axis=0)
    packet = lax.dot_general(
        pick_mask.astype(F32), carried, (((1,), (1,)), ((), ())), precision=lax.Precision.HIGHEST,
        preferred_element_type=F32,
    )
    arrived = swap(packet, -1, face, 0)[:, :8]
    moves = []
    for d in range(8):
        ds, db = DIRECTIONS[d]
        moves += [(db * span, 0.0, ds * span)] * (face if d < 4 else EDGE)
    ghost_pos = arrived[:, :3] + jnp.array(moves, F32)
    ghost_hot = (arrived[:, 3:4] == kinds.astype(F32)[None, :]).astype(BF16)
    ext_start = jnp.dot(
        jnp.concatenate([onehot, ghost_hot], axis=0), embedding, preferred_element_type=F32
    ).astype(BF16)
    ext_pos = jnp.pad(jnp.concatenate([positions, ghost_pos.T], axis=1), ((0, 5), (0, 0)))
    own = jnp.tile(jnp.pad(positions, ((0, 5), (0, 0))), (1, GROUP))

    past = neighbour_slot - first_edge
    slots = jnp.where(past >= 0, first_edge + (past // edge) * EDGE + past % edge, neighbour_slot)
    slots = slots.T.reshape(steps, 1, lanes)
    live = (jnp.arange(slot_count)[:, None] < neighbour_count[None, :]).astype(F32)
    live = (live / math.sqrt(slot_count)).reshape(steps, 1, lanes)

    select_one = jnp.dot(onehot, product_weight[0], preferred_element_type=F32)
    select_two = jnp.dot(onehot, product_weight[1], preferred_element_type=F32)
    gates = jnp.dot(onehot, equi_weight, preferred_element_type=F32)
    w1 = jnp.pad(radial_first, ((0, 0), (0, 8), (0, 0)))
    w1t = w1.transpose(0, 2, 1)
    wht = radial_hidden.transpose(0, 1, 3, 2)
    rad = radial_hidden.shape[-1]

    def struct(shape, dtype):
        return jax.ShapeDtypeStruct(shape, dtype)

    def common(feature_width, paths):
        return [
            pltpu.VMEM((steps, rows, lanes), BF16),
            pltpu.VMEM((steps, 8, lanes), F32),
            pltpu.VMEM((steps, 16, lanes), F32),
            pltpu.VMEM((steps, 3, rad, lanes), F32),
            pltpu.VMEM((steps, lanes, feature_width), BF16),
            pltpu.VMEM((steps, lanes, paths * channels), BF16),
            pltpu.VMEM((lanes, 9 * channels), F32),
        ]

    mom, layer_one, packets, *kept = call(
        functools.partial(first_forward, steps),
        "layer_one_forward",
        (slots, live, own, ext_pos, ext_start, w1t[0], wht[0], radial_last_one, select_one, gates,
         mix_weight[0], skip_weight[0], equi_mix, pick),
        [struct((9, atoms, channels), F32), struct((atoms, 9 * channels), BF16), struct((ghosts, 9 * channels), BF16)]
        + [struct((steps, 8, lanes), F32), struct((steps, 16, lanes), F32), struct((steps, 3, rad, lanes), F32),
           struct((steps, lanes, channels), BF16), struct((steps, lanes, 3 * channels), BF16)],
        [pltpu.VMEM((steps, rows, lanes), BF16), pltpu.VMEM((lanes, 9 * channels), F32)],
    )
    ghost_one = swap(packets, -1, face, 1)
    moment_scratch = pltpu.VMEM((9, atoms, channels), F32)
    energy, gown, gpackets, posown, posext = call(
        functools.partial(second_both, steps),
        "layer_two",
        (slots, live, own, ext_pos, layer_one, ghost_one, w1t[1], w1[1], wht[1], radial_hidden[1], radial_last_two, select_two,
         mix_weight[1], skip_weight[1], readout_weight.astype(F32)[None], head_weight, final_weight.astype(F32)[None]),
        [struct((atoms, 1), F32), struct((atoms, 9 * channels), F32), struct((ghosts, 9 * channels), BF16),
         struct((8, atoms), F32), struct((8, rows), F32)],
        common(9 * channels, 7)
        + [moment_scratch, pltpu.VMEM((lanes, 7 * channels), BF16)]
        + [pltpu.VMEM((lanes, 8 * channels), BF16)] * 2
        + [pltpu.VMEM((lanes, 9 * channels), BF16), pltpu.VMEM((rows, 9 * channels), BF16)]
        + [pltpu.VMEM((rows, 9 * channels), F32)],
    )
    returned = swap(gpackets, 1, face, 2)
    posown, posext = call(
        functools.partial(first_backward, steps),
        "layer_one_backward",
        (slots, live, ext_start, w1[0], radial_hidden[0], radial_last_one, select_one,
         gates, mix_weight[0], skip_weight[0], equi_mix, pick, mom, gown, returned, posown, posext, *kept),
        [struct((8, atoms), F32), struct((8, rows), F32)],
        [pltpu.VMEM((rows, lanes), BF16), pltpu.VMEM((lanes, 9 * channels), F32)]
        + [moment_scratch, pltpu.VMEM((lanes, 3 * channels), BF16)]
        + [pltpu.VMEM((lanes, 8 * channels), BF16)] * 2,
    )
    back = jnp.pad(posext[:, atoms:].T, ((0, 0), (0, channels - 8)))
    back = swap(back, 1, face, 3)[:, :8]
    gathered = lax.dot_general(
        back, pick_mask.astype(F32), TN, precision=lax.Precision.HIGHEST, preferred_element_type=F32
    )
    total = posown + posext[:, :atoms] + gathered
    base = jnp.sum(jnp.where(species[:, None] == kinds[None, :], atom_reference[None, :], 0.0), axis=1)
    return (base + energy[:, 0], -total[:3])


def solution(mesh):
    every = ("slab", "brick")
    placed = (P(None, every), P(every), P(every, None), P(every), P(every, None, None), P(every, None, None))
    placed = placed + (P(),) * 14
    return jax.shard_map(
        shards, mesh=mesh, in_specs=placed, out_specs=(P(every), P(None, every)), check_vma=False
    )
```
